512 devices in a mesh: node: 8 (over z), outer: 64 (over x, y, core).
Axes of the slice: x: 4, y: 8, z: 8, core: 2. Of those that a mesh axis runs over, the one named last changes fastest.
Arguments:
- tokens: bfloat16 [16384, 2048], P('outer', 'node'), may hold values from -6 to 6
- cotangent: bfloat16 [16384, 2048], P('outer', 'node'), may hold values from -6 to 6
- gate: float32 [16384], P('outer'), may hold values from 0.2 to 1
- expert_ids: int32 [16384, 1], P('outer'), may hold values from 0 to 63; in each aligned block of 256 rows (0 to 255, 256 to 511, ...) at most 8 rows name the same one
- dense_in: bfloat16 [2048, 4096], P('outer', 'node'), may hold values from -0.125 to 0.125
- dense_out: bfloat16 [4096, 2048], P('node', 'outer'), may hold values from -0.09375 to 0.09375
- expert_in: bfloat16 [64, 2048, 4096], P('outer', None, 'node'), may hold values from -0.125 to 0.125
- expert_out: bfloat16 [64, 4096, 2048], P('outer', 'node'), may hold values from -0.09375 to 0.09375
Outputs:
- mixed: bfloat16 [16384, 2048], P('outer', 'node')
- input_grad: bfloat16 [16384, 2048], P('outer', 'node')
The draws below stay inside these ranges and needn't reach their ends.
Inputs may be any that keep to these rules, and one draw needn't show every extreme that they name: `expert_ids`: within the tokens of one index of outer (aligned blocks of 256 rows) no expert is named by more than 8 tokens, and in some blocks one is named by exactly 8; every expert is named somewhere.
All inputs are finite; a program needn't handle non-finite values.
Results may differ from the reference program's by a relative error of at most 0.015.
Values may be sent and summed in bfloat16 or wider, within the bound.
No kernel may reach another device: no remote copies, remote signals or barrier semaphores. Data moves between devices by JAX's collectives and lax.ppermute only.
A program may use at most 64 MiB of HBM per device.

```python
import math
import jax
import jax.numpy as jnp
import numpy as np
from jax import lax

D = 2048
DENSE_FF = 4096
EXP_FF = 4096
TOK_OUT = 256
EXPERTS = 64
CAP = 8
TOKENS = 16384
N_NODE = 8
N_OUTER = 64


def shard_levels(rng, dims, split, least, largest):
    factor_of = 1.0
    for position, blocks in split:
        draws = jax.random.uniform(jax.random.fold_in(jax.random.fold_in(rng, 6), position), (blocks,), jnp.float32, least / len(split), largest / len(split))
        factor_of = factor_of * jnp.repeat(jnp.exp(draws), dims[position] // blocks).reshape((-1,) + (1,) * (len(dims) - 1 - position))
    return factor_of


def shared_out(own_key, own, number, rows, number_of, top, bound, lean):
    sequence = jax.random.permutation(own_key, number_of)
    crowded, usual = shares(number_of, rows * top, bound, lean, True), shares(number_of, rows * top, bound, lean, False)
    places = jnp.arange(number_of)

    def named(sizes, rotation):
        used = int((sizes > 0).sum())
        fixed = max(1, used // 4)
        passed = fixed + (places - fixed + rotation * (used - fixed)) % max(1, number_of - fixed)
        return jnp.zeros((number_of,), jnp.int32).at[sequence[jnp.where(places < fixed, places, passed)]].set(jnp.asarray(sizes, jnp.int32))

    sizes = jnp.where(number % 4 == 0, named(crowded, number // 4), named(usual, number - number // 4 - 1))
    mixed = jax.random.permutation(jax.random.fold_in(own, 3), number_of)
    donor, sink = mixed[0:number_of // 2 * 2:2], mixed[1:number_of // 2 * 2:2]
    margin = jnp.minimum(sizes[donor] - 1, bound - sizes[sink]) // 2
    margin = jnp.where((donor == sequence[0]) | (sink == sequence[0]) | (sizes[sink] == 0), 0, jnp.maximum(margin, 0))
    passed = jax.random.randint(jax.random.fold_in(own, 4), (number_of // 2,), 0, 1 << 20) % (margin + 1)
    sizes = sizes.at[donor].add(-passed).at[sink].add(passed)
    items = jnp.searchsorted(jnp.cumsum(sizes), jnp.arange(rows * top), side="right").astype(jnp.int32)
    listing = items.reshape(top, rows).T
    listing = listing[jax.random.permutation(jax.random.fold_in(own, 1), rows)]
    rotation = jax.random.randint(jax.random.fold_in(own, 2), (rows, 1), 0, top)
    return jnp.take_along_axis(listing, (jnp.arange(top)[None, :] + rotation) % top, axis=1)


def shares(number_of, total, bound, lean, full):
    loads = [(1 << 20) // math.isqrt(standing ** lean) + 1 for standing in range(1, number_of + 1)]
    largest = bound if full else min(bound, max(-(-total // number_of), total * loads[0] // sum(loads)))
    least = 1 if total - largest >= number_of - 1 else 0
    counts, surplus = [largest] + [least] * (number_of - 1), total - largest - least * (number_of - 1)
    while surplus > 0:
        candidates = [i for i in range(1, number_of) if counts[i] < largest] or [i for i in range(1, number_of) if counts[i] < bound]
        whole, budget = sum([loads[i] for i in candidates]), surplus
        for i in candidates:
            extra = min(bound - counts[i], max(1, budget * loads[i] // whole), surplus)
            counts[i] = counts[i] + extra
            surplus = surplus - extra
    return np.array(counts)


def normal_values(stream_key, dims, spread, most, cuts=(), kind=jnp.bfloat16):
    factor_of = shard_levels(stream_key, dims, cuts, -0.22, 0.18) if cuts else 1.0
    entries = jax.random.normal(stream_key, dims, jnp.float32) * spread * factor_of
    return jnp.minimum(jnp.maximum(entries, -most), most).astype(kind)


def setup_inputs(seed: int = 0) -> dict:
    streams_of = jax.random.split(jax.random.key(seed), 9)
    tokens = normal_values(streams_of[0], (TOKENS, D), 1.0, 6.0, ((0, 64), (1, 8)))
    cotangent = normal_values(streams_of[1], (TOKENS, D), 1.0, 6.0, ((0, 64), (1, 8)))
    gate = jnp.clip(jnp.exp(math.log(1.0) - 1.609438 * jax.random.uniform(streams_of[2], (TOKENS,), jnp.float32) ** shard_levels(streams_of[2], (TOKENS,), ((0, 64),), -0.2, 0.2)), 0.2, 1.0)
    expert_ids_keys = jax.random.split(jax.random.fold_in(streams_of[3], 1), TOKENS // TOK_OUT)
    expert_ids_turns = jax.random.permutation(jax.random.fold_in(streams_of[3], 3), TOKENS // TOK_OUT)
    expert_ids = jax.vmap(lambda own, number: shared_out(jax.random.fold_in(streams_of[3], 2), own, number, TOK_OUT, EXPERTS, 1, CAP, 2))(expert_ids_keys, expert_ids_turns).reshape((TOKENS, 1))
    dense_in = normal_values(streams_of[4], (D, DENSE_FF), D ** -0.5, 0.125, ((0, 64), (1, 8)))
    dense_out = normal_values(streams_of[5], (DENSE_FF, D), DENSE_FF ** -0.5, 0.09375, ((0, 8), (1, 64)))
    expert_in = normal_values(streams_of[6], (EXPERTS, D, EXP_FF), D ** -0.5, 0.125, ((0, 64), (2, 8)))
    expert_out = normal_values(streams_of[7], (EXPERTS, EXP_FF, D), EXP_FF ** -0.5, 0.09375, ((0, 64), (1, 8)))
    return dict(tokens=tokens, cotangent=cotangent, gate=gate, expert_ids=expert_ids, dense_in=dense_in, dense_out=dense_out, expert_in=expert_in, expert_out=expert_out)


def gelu_value(v):
    return 0.5 * v * (1.0 + lax.erf(v * 0.7071067811865476))


def gelu_prime(v):
    return 0.5 * (1.0 + lax.erf(v * 0.7071067811865476)) + v * jnp.exp(-0.5 * v * v) * 0.3989422804014327


def slot_table(expert_ids):
    blocks = expert_ids[:, 0].reshape(N_OUTER, TOK_OUT).astype(jnp.int32)
    labels = jnp.arange(EXPERTS, dtype=jnp.int32)
    onehot = (blocks[:, :, None] == labels[None, None, :]).astype(jnp.int32)
    ranks = jnp.cumsum(onehot, axis=1) - 1
    own_rank = jnp.sum(ranks * onehot, axis=2).astype(jnp.int32)
    return (blocks * CAP + own_rank).astype(jnp.int32)


def expert_work(inputs):
    rows_x, rows_c, weight_in, weight_out = inputs
    block = EXP_FF // N_NODE
    pre_act = jnp.dot(rows_x, weight_in, preferred_element_type=jnp.float32)
    hidden = gelu_value(pre_act).astype(jnp.bfloat16)
    hidden_split = hidden.astype(jnp.float32).reshape(-1, N_NODE, block)
    out_split = weight_out.astype(jnp.float32).reshape(N_NODE, block, D)
    parts = jnp.einsum('rnh,nhd->nrd', hidden_split, out_split).astype(jnp.bfloat16)
    summed_out = jnp.sum(parts.astype(jnp.float32), axis=0)
    grad_hid = lax.dot_general(rows_c, weight_out, (((1,), (1,)), ((), ())), preferred_element_type=jnp.float32)
    dpre = (grad_hid * gelu_prime(pre_act)).astype(jnp.bfloat16)
    dpre_split = dpre.astype(jnp.float32).reshape(-1, N_NODE, block)
    in_split = weight_in.astype(jnp.float32).reshape(D, N_NODE, block)
    back_parts = jnp.einsum('rnh,dnh->nrd', dpre_split, in_split).astype(jnp.bfloat16)
    summed_back = jnp.sum(back_parts.astype(jnp.float32), axis=0)
    return summed_out, summed_back


def reference(tokens, cotangent, gate, expert_ids, dense_in, dense_out, expert_in, expert_out):
    dense_pre = jnp.dot(tokens, dense_in, preferred_element_type=jnp.float32)
    dense_hidden = gelu_value(dense_pre).astype(jnp.bfloat16)
    dense_fwd = jnp.dot(dense_hidden, dense_out, preferred_element_type=jnp.float32)
    dense_grad = lax.dot_general(cotangent, dense_out, (((1,), (1,)), ((), ())), preferred_element_type=jnp.float32)
    dense_dpre = (dense_grad * gelu_prime(dense_pre)).astype(jnp.bfloat16)
    dense_bwd = lax.dot_general(dense_dpre, dense_in, (((1,), (1,)), ((), ())), preferred_element_type=jnp.float32)

    slots = slot_table(expert_ids)
    tok_blocks = tokens.reshape(N_OUTER, TOK_OUT, D)
    cot_blocks = cotangent.reshape(N_OUTER, TOK_OUT, D)

    def place(slot_row, values):
        return jnp.zeros((EXPERTS * CAP, D), values.dtype).at[slot_row].set(values)

    buf_x = jax.vmap(place)(slots, tok_blocks).reshape(N_OUTER, EXPERTS, CAP, D)
    buf_c = jax.vmap(place)(slots, cot_blocks).reshape(N_OUTER, EXPERTS, CAP, D)
    rows_x = jnp.transpose(buf_x, (1, 0, 2, 3)).reshape(EXPERTS, N_OUTER * CAP, D)
    rows_c = jnp.transpose(buf_c, (1, 0, 2, 3)).reshape(EXPERTS, N_OUTER * CAP, D)
    result_out, result_back = lax.map(expert_work, (rows_x, rows_c, expert_in, expert_out))

    def unplace(result):
        per_block = jnp.transpose(result.reshape(EXPERTS, N_OUTER, CAP, D), (1, 0, 2, 3)).reshape(N_OUTER, EXPERTS * CAP, D)
        picked = jax.vmap(lambda table, slot_row: jnp.take(table, slot_row, axis=0))(per_block, slots)
        return picked.reshape(TOKENS, D)

    routed_out = unplace(result_out)
    routed_back = unplace(result_back)
    weight = gate.astype(jnp.float32)[:, None]
    mixed = (tokens.astype(jnp.float32) + dense_fwd + weight * routed_out).astype(jnp.bfloat16)
    input_grad = (cotangent.astype(jnp.float32) + dense_bwd + weight * routed_back).astype(jnp.bfloat16)
    return mixed, input_grad
```

```python
import jax
import jax.numpy as jnp
from jax import lax
from jax.sharding import PartitionSpec as P


def gelu_value(v):
    return 0.5 * v * (1.0 + lax.erf(v * 0.7071067811865476))


def gelu_prime(v):
    return (
        0.5 * (1.0 + lax.erf(v * 0.7071067811865476))
        + v * jnp.exp(-0.5 * v * v) * 0.3989422804014327
    )


def dot(left, right):
    return jnp.dot(left, right, preferred_element_type=jnp.float32)


def contract_last(left, right):
    return lax.dot_general(
        left, right, (((1,), (1,)), ((), ())), preferred_element_type=jnp.float32
    )


def body(tokens, cotangent, gate, expert_ids, dense_in, dense_out, expert_in, expert_out):
    bf16, f32 = jnp.bfloat16, jnp.float32
    n_node, n_outer = lax.axis_size("node"), lax.axis_size("outer")
    z = lax.axis_index("node").astype(jnp.uint32)
    tok_count, feat = tokens.shape
    experts = n_outer * expert_in.shape[0]
    capacity = max(2, 2 * tok_count // n_outer)
    slots = experts * capacity

    def to_right(a):
        return lax.ppermute(a, "node", [(i, (i + 1) % n_node) for i in range(n_node)])

    def to_left(a):
        return lax.ppermute(a, "node", [(i, (i - 1) % n_node) for i in range(n_node)])

    both = jnp.concatenate([tokens, cotangent], axis=0)
    dense_rows = lax.all_gather(both, "node", axis=1, tiled=True)
    weights = lax.all_gather(
        jnp.stack([dense_in, dense_out.T]), "outer", axis=1, tiled=True
    )

    routed = expert_ids[:, 0]
    labels = jnp.arange(experts, dtype=jnp.int32)
    onehot = (routed[:, None] == labels[None, :]).astype(bf16)
    order = jnp.arange(tok_count, dtype=jnp.int32)
    before = (order[:, None] > order[None, :]).astype(bf16)
    ranks = jnp.sum(dot(before, onehot) * onehot.astype(f32), axis=1).astype(jnp.int32)
    slot_of = routed * capacity + ranks
    place = (jnp.arange(slots, dtype=jnp.int32)[:, None] == slot_of[None, :]).astype(bf16)

    send = dot(place, jnp.concatenate([tokens, cotangent], axis=1)).astype(bf16)
    send = jnp.concatenate(
        [
            send[:, :feat].reshape(n_outer, capacity, feat),
            send[:, feat:].reshape(n_outer, capacity, feat),
        ],
        axis=1,
    )
    own = lax.all_to_all(send, "outer", split_axis=0, concat_axis=0, tiled=True)
    own = jnp.concatenate(
        [own[:, :capacity].reshape(slots, feat), own[:, capacity:].reshape(slots, feat)], axis=0
    )

    w_in, w_out = expert_in[0], expert_out[0]

    zero = jnp.uint32(0)

    def start_of(offset):
        return lax.rem(z + jnp.uint32(offset + n_node), jnp.uint32(n_node)) * jnp.uint32(feat)

    def in_slice(offset):
        return lax.dynamic_slice(w_in, (start_of(offset), zero), (feat, w_in.shape[1]))

    def out_slice(offset):
        return lax.dynamic_slice(w_out, (zero, start_of(offset)), (w_out.shape[0], feat))

    half = n_node // 2
    w_ins = {o: in_slice(o) for o in range(-half + 1, half + 1)}
    w_outs = {o: out_slice(o) for o in range(-half + 1, half + 1)}

    pre = dot(own[:slots], w_ins[0])
    grad = contract_last(own[slots:], w_outs[0])
    from_left = from_right = own
    for step in range(1, half):
        from_left, from_right = to_right(from_left), to_left(from_right)
        pre = pre + dot(from_left[:slots], w_ins[-step])
        grad = grad + contract_last(from_left[slots:], w_outs[-step])
        pre = pre + dot(from_right[:slots], w_ins[step])
        grad = grad + contract_last(from_right[slots:], w_outs[step])
    last_x, last_c = to_right(from_left[:slots]), to_left(from_right[slots:])
    pre = pre + dot(last_x, w_ins[half])
    grad = grad + contract_last(last_c, w_outs[half])

    hidden = gelu_value(pre).astype(bf16)
    dpre = (grad * gelu_prime(pre)).astype(bf16)

    def part_out(offset):
        return dot(hidden, w_outs[offset])

    def part_back(offset):
        return contract_last(dpre, w_ins[offset])

    r_out = to_right(part_out(half).astype(bf16))
    l_back = to_left(part_back(half).astype(bf16))
    r_back = l_out = None
    for step in range(half - 1, 0, -1):
        ro, rb = part_out(step), part_back(step)
        lo, lb = part_out(-step), part_back(-step)
        ro = ro + r_out.astype(f32)
        lb = lb + l_back.astype(f32)
        if r_back is not None:
            rb = rb + r_back.astype(f32)
            lo = lo + l_out.astype(f32)
        right = to_right(jnp.concatenate([ro.astype(bf16), rb.astype(bf16)], axis=0))
        left = to_left(jnp.concatenate([lo.astype(bf16), lb.astype(bf16)], axis=0))
        r_out, r_back = right[:slots], right[slots:]
        l_out, l_back = left[:slots], left[slots:]
    sum_out = part_out(0) + r_out.astype(f32) + l_out.astype(f32)
    sum_back = part_back(0) + r_back.astype(f32) + l_back.astype(f32)
    reply = jnp.concatenate(
        [
            sum_out.astype(bf16).reshape(n_outer, capacity, feat),
            sum_back.astype(bf16).reshape(n_outer, capacity, feat),
        ],
        axis=1,
    )
    reply = lax.all_to_all(reply, "outer", split_axis=0, concat_axis=0, tiled=True)

    dense_x, dense_c = dense_rows[:tok_count], dense_rows[tok_count:]
    weight_in, weight_out = weights[0], weights[1]
    dense_pre = dot(dense_x, weight_in)
    dense_hidden = gelu_value(dense_pre).astype(bf16)
    dense_grad = dot(dense_c, weight_out)
    dense_dpre = (dense_grad * gelu_prime(dense_pre)).astype(bf16)
    dense_sum = lax.psum_scatter(
        jnp.concatenate(
            [
                contract_last(dense_hidden, weight_out).astype(bf16),
                contract_last(dense_dpre, weight_in).astype(bf16),
            ],
            axis=0,
        ),
        "node",
        scatter_dimension=1,
        tiled=True,
    ).astype(f32)

    picked_out = lax.dot_general(
        place,
        reply[:, :capacity].reshape(slots, feat),
        (((0,), (0,)), ((), ())),
        preferred_element_type=f32,
    )
    picked_back = lax.dot_general(
        place,
        reply[:, capacity:].reshape(slots, feat),
        (((0,), (0,)), ((), ())),
        preferred_element_type=f32,
    )
    weight = gate[:, None]
    mixed = tokens.astype(f32) + dense_sum[:tok_count] + weight * picked_out
    input_grad = cotangent.astype(f32) + dense_sum[tok_count:] + weight * picked_back
    return mixed.astype(bf16), input_grad.astype(bf16)


def solution(mesh):
    placed = (
        P("outer", "node"),
        P("outer", "node"),
        P("outer"),
        P("outer", None),
        P("outer", "node"),
        P("node", "outer"),
        P("outer", None, "node"),
        P("outer", "node", None),
    )
    return jax.shard_map(
        body,
        mesh=mesh,
        in_specs=placed,
        out_specs=(P("outer", "node"), P("outer", "node")),
        check_vma=False,
    )
```

```python
import jax
import jax.numpy as jnp
from jax import lax
from jax.sharding import PartitionSpec as P


def gelu_value(v):
    return 0.5 * v * (1.0 + lax.erf(v * 0.7071067811865476))


def gelu_prime(v):
    return (
        0.5 * (1.0 + lax.erf(v * 0.7071067811865476))
        + v * jnp.exp(-0.5 * v * v) * 0.3989422804014327
    )


def dot(left, right):
    return jnp.dot(left, right, preferred_element_type=jnp.float32)


def contract_last(left, right):
    return lax.dot_general(
        left, right, (((1,), (1,)), ((), ())), preferred_element_type=jnp.float32
    )


def body(tokens, cotangent, gate, expert_ids, dense_in, dense_out, expert_in, expert_out):
    bf16, f32 = jnp.bfloat16, jnp.float32
    n_node, n_outer = lax.axis_size("node"), lax.axis_size("outer")
    z = lax.axis_index("node").astype(jnp.uint32)
    tok_count, feat = tokens.shape
    experts = n_outer * expert_in.shape[0]
    capacity = max(2, 2 * tok_count // n_outer)
    slots = experts * capacity

    def to_right(a):
        return lax.ppermute(a, "node", [(i, (i + 1) % n_node) for i in range(n_node)])

    def to_left(a):
        return lax.ppermute(a, "node", [(i, (i - 1) % n_node) for i in range(n_node)])

    zero = jnp.uint32(0)
    dense_right = to_right(jnp.concatenate([tokens, cotangent], axis=0))
    dense_left = to_left(jnp.concatenate([cotangent, tokens], axis=0))

    routed = expert_ids[:, 0]
    labels = jnp.arange(experts, dtype=jnp.int32)
    onehot = (routed[:, None] == labels[None, :]).astype(bf16)
    order = jnp.arange(tok_count, dtype=jnp.int32)
    before = (order[:, None] > order[None, :]).astype(bf16)
    ranks = jnp.sum(dot(before, onehot) * onehot.astype(f32), axis=1).astype(jnp.int32)
    slot_of = routed * capacity + ranks
    place = (jnp.arange(slots, dtype=jnp.int32)[:, None] == slot_of[None, :]).astype(bf16)

    send = dot(place, jnp.concatenate([tokens, cotangent], axis=1)).astype(bf16)
    send = jnp.concatenate(
        [
            send[:, :feat].reshape(n_outer, capacity, feat),
            send[:, feat:].reshape(n_outer, capacity, feat),
        ],
        axis=1,
    )
    own = lax.all_to_all(send, "outer", split_axis=0, concat_axis=0, tiled=True)
    own = jnp.concatenate(
        [own[:, :capacity].reshape(slots, feat), own[:, capacity:].reshape(slots, feat)], axis=0
    )
    own, dense_right, dense_left = lax.optimization_barrier((own, dense_right, dense_left))
    rows = lax.all_gather(own, "node", axis=1, tiled=True)

    depth, width = dense_in.shape
    pieces = jnp.concatenate([dense_in, dense_out.T], axis=0)
    pieces = jnp.stack([pieces[:, : width // 2], pieces[:, width // 2 :]])
    pieces, own = lax.optimization_barrier((pieces, own))
    pieces = jnp.broadcast_to(pieces, (n_outer // 2,) + pieces.shape)
    near = lax.all_to_all(
        pieces.reshape(n_outer, 2 * depth, width // 2),
        "outer",
        split_axis=0,
        concat_axis=0,
        tiled=True,
    )

    def dense_up(half_weights):
        w_i = half_weights[:, :depth].reshape(n_outer * depth, width // 2)
        w_o = half_weights[:, depth:].reshape(n_outer * depth, width // 2)
        pre_d = dot(dense_rows[:tok_count], w_i)
        grad_d = dot(dense_rows[tok_count:], w_o)
        return (
            w_i,
            w_o,
            gelu_value(pre_d).astype(bf16),
            (grad_d * gelu_prime(pre_d)).astype(bf16),
        )

    def start_of(offset):
        return lax.rem(z + jnp.uint32(offset + n_node), jnp.uint32(n_node)) * jnp.uint32(feat)

    half = n_node // 2
    dense_rows = jnp.zeros((2 * tok_count, n_node * feat), bf16)

    def put(array, values, offset, row):
        return lax.dynamic_update_slice(array, values, (jnp.uint32(row), start_of(offset)))

    def put_pair(array, from_left, from_right, hop):
        array = put(array, from_left, -hop, 0)
        array = put(array, from_right[:tok_count], hop, tok_count)
        return put(array, from_right[tok_count:], hop, 0)

    dense_rows = put(dense_rows, tokens, 0, 0)
    dense_rows = put(dense_rows, cotangent, 0, tok_count)
    dense_rows = put_pair(dense_rows, dense_right, dense_left, 1)
    dense_right, dense_left = to_right(dense_right), to_left(dense_left)
    for hop in range(2, half):
        dense_rows = put_pair(dense_rows, dense_right, dense_left, hop)
        if hop == half - 1:
            dense_right, dense_left = dense_right[:tok_count], dense_left[:tok_count]
        dense_right, dense_left = to_right(dense_right), to_left(dense_left)
    dense_rows = put(dense_rows, dense_right, half, 0)
    dense_rows = put(dense_rows, dense_left, half, tok_count)

    far = lax.ppermute(near, "outer", [(i, i ^ 1) for i in range(n_outer)])
    dense = dense_up(near)
    rows, dense = lax.optimization_barrier((rows, dense))
    w_in, w_out = expert_in[0], expert_out[0]
    pre = dot(rows[:slots], w_in)
    grad = contract_last(rows[slots:], w_out)
    back = contract_last((grad * gelu_prime(pre)).astype(bf16), w_in).astype(bf16)
    hidden = gelu_value(pre).astype(bf16)

    def part_out(offset):
        weights = lax.dynamic_slice(w_out, (zero, start_of(offset)), (w_out.shape[0], feat))
        return dot(hidden, weights)

    mid = slots // 2
    first = part_out(half).astype(bf16)
    back, first, far, dense_rows = lax.optimization_barrier((back, first, far, dense_rows))
    sum_back = lax.psum_scatter(back, "node", scatter_dimension=1, tiled=True)
    right, left = to_right(first[:mid]), to_left(first[mid:])
    for step in range(half - 1, 0, -1):
        ro, lo = part_out(step), part_out(-step)
        if step == half - 1:
            ro = jnp.concatenate([ro[:mid] + right.astype(f32), ro[mid:]], axis=0)
            lo = jnp.concatenate([lo[:mid], lo[mid:] + left.astype(f32)], axis=0)
        else:
            ro, lo = ro + right.astype(f32), lo + left.astype(f32)
        right, left = ro.astype(bf16), lo.astype(bf16)
        if step == half - 1:
            wi_n, wo_n, hid_n, dpre_n = dense
            wi_f, wo_f, hid_f, dpre_f = dense_up(far)
            right, left, hid_f, dpre_f = lax.optimization_barrier((right, left, hid_f, dpre_f))
        elif step == half - 2:
            dense = jnp.concatenate(
                [
                    contract_last(hid_n, wo_n) + contract_last(hid_f, wo_f),
                    contract_last(dpre_n, wi_n) + contract_last(dpre_f, wi_f),
                ],
                axis=0,
            ).astype(bf16)
            right, left, dense = lax.optimization_barrier((right, left, dense))
        right, left = to_right(right), to_left(left)
    sum_out = (part_out(0) + right.astype(f32) + left.astype(f32)).astype(bf16)
    dense_sum = lax.psum_scatter(dense, "node", scatter_dimension=1, tiled=True).astype(f32)

    reply = jnp.concatenate(
        [
            sum_out.reshape(n_outer, capacity, feat),
            sum_back.reshape(n_outer, capacity, feat),
        ],
        axis=1,
    )
    reply = lax.all_to_all(reply, "outer", split_axis=0, concat_axis=0, tiled=True)

    picked_out = lax.dot_general(
        place,
        reply[:, :capacity].reshape(slots, feat),
        (((0,), (0,)), ((), ())),
        preferred_element_type=f32,
    )
    picked_back = lax.dot_general(
        place,
        reply[:, capacity:].reshape(slots, feat),
        (((0,), (0,)), ((), ())),
        preferred_element_type=f32,
    )
    scale = gate[:, None]
    mixed = tokens.astype(f32) + dense_sum[:tok_count] + scale * picked_out
    input_grad = cotangent.astype(f32) + dense_sum[tok_count:] + scale * picked_back
    return mixed.astype(bf16), input_grad.astype(bf16)


def solution(mesh):
    placed = (
        P("outer", "node"),
        P("outer", "node"),
        P("outer"),
        P("outer", None),
        P("outer", "node"),
        P("node", "outer"),
        P("outer", None, "node"),
        P("outer", "node", None),
    )
    return jax.shard_map(
        body,
        mesh=mesh,
        in_specs=placed,
        out_specs=(P("outer", "node"), P("outer", "node")),
        check_vma=False,
    )
```

```python
import jax
import jax.numpy as jnp
from jax import lax
from jax.sharding import PartitionSpec as P


def gelu_value(v):
    return 0.5 * v * (1.0 + lax.erf(v * 0.7071067811865476))


def gelu_prime(v):
    return (
        0.5 * (1.0 + lax.erf(v * 0.7071067811865476))
        + v * jnp.exp(-0.5 * v * v) * 0.3989422804014327
    )


def dot(left, right):
    return jnp.dot(left, right, preferred_element_type=jnp.float32)


def contract_last(left, right):
    return lax.dot_general(
        left, right, (((1,), (1,)), ((), ())), preferred_element_type=jnp.float32
    )


def body(tokens, cotangent, gate, expert_ids, dense_in, dense_out, expert_in, expert_out):
    bf16, f32 = jnp.bfloat16, jnp.float32
    n_node, n_outer = lax.axis_size("node"), lax.axis_size("outer")
    z = lax.axis_index("node").astype(jnp.uint32)
    tok_count, feat = tokens.shape
    experts = n_outer * expert_in.shape[0]
    capacity = max(2, 2 * tok_count // n_outer)
    slots = experts * capacity

    def to_right(a):
        return lax.ppermute(a, "node", [(i, (i + 1) % n_node) for i in range(n_node)])

    def to_left(a):
        return lax.ppermute(a, "node", [(i, (i - 1) % n_node) for i in range(n_node)])

    zero = jnp.uint32(0)
    dense_right = to_right(jnp.concatenate([tokens, cotangent], axis=0))
    dense_left = to_left(jnp.concatenate([cotangent, tokens], axis=0))

    routed = expert_ids[:, 0]
    labels = jnp.arange(experts, dtype=jnp.int32)
    onehot = (routed[:, None] == labels[None, :]).astype(bf16)
    order = jnp.arange(tok_count, dtype=jnp.int32)
    before = (order[:, None] > order[None, :]).astype(bf16)
    ranks = jnp.sum(dot(before, onehot) * onehot.astype(f32), axis=1).astype(jnp.int32)
    slot_of = routed * capacity + ranks
    place = (jnp.arange(slots, dtype=jnp.int32)[:, None] == slot_of[None, :]).astype(bf16)

    send = dot(place, jnp.concatenate([tokens, cotangent], axis=1)).astype(bf16)
    send = jnp.concatenate(
        [
            send[:, :feat].reshape(n_outer, capacity, feat),
            send[:, feat:].reshape(n_outer, capacity, feat),
        ],
        axis=1,
    )
    own = lax.all_to_all(send, "outer", split_axis=0, concat_axis=0, tiled=True)
    own = jnp.concatenate(
        [own[:, :capacity].reshape(slots, feat), own[:, capacity:].reshape(slots, feat)], axis=0
    )
    own, dense_right, dense_left = lax.optimization_barrier((own, dense_right, dense_left))
    rows = lax.all_gather(own, "node", axis=1, tiled=True)

    depth, width = dense_in.shape
    pieces = jnp.concatenate([dense_in, dense_out.T], axis=0)
    pieces = jnp.stack([pieces[:, : width // 2], pieces[:, width // 2 :]])
    pieces, own = lax.optimization_barrier((pieces, own))
    pieces = jnp.broadcast_to(pieces, (n_outer // 2,) + pieces.shape)
    near = lax.all_to_all(
        pieces.reshape(n_outer, 2 * depth, width // 2),
        "outer",
        split_axis=0,
        concat_axis=0,
        tiled=True,
    )

    def dense_up(half_weights):
        w_i = half_weights[:, :depth].reshape(n_outer * depth, width // 2)
        w_o = half_weights[:, depth:].reshape(n_outer * depth, width // 2)
        pre_d = dot(dense_rows[:tok_count], w_i)
        grad_d = dot(dense_rows[tok_count:], w_o)
        return (
            w_i,
            w_o,
            gelu_value(pre_d).astype(bf16),
            (grad_d * gelu_prime(pre_d)).astype(bf16),
        )

    def start_of(offset):
        return lax.rem(z + jnp.uint32(offset + n_node), jnp.uint32(n_node)) * jnp.uint32(feat)

    half = n_node // 2
    dense_rows = jnp.zeros((2 * tok_count, n_node * feat), bf16)

    def put(array, values, offset, row):
        return lax.dynamic_update_slice(array, values, (jnp.uint32(row), start_of(offset)))

    def put_pair(array, from_left, from_right, hop):
        array = put(array, from_left, -hop, 0)
        array = put(array, from_right[:tok_count], hop, tok_count)
        return put(array, from_right[tok_count:], hop, 0)

    dense_rows = put(dense_rows, tokens, 0, 0)
    dense_rows = put(dense_rows, cotangent, 0, tok_count)
    dense_rows = put_pair(dense_rows, dense_right, dense_left, 1)
    dense_right, dense_left = to_right(dense_right), to_left(dense_left)
    for hop in range(2, half):
        dense_rows = put_pair(dense_rows, dense_right, dense_left, hop)
        if hop == half - 1:
            dense_right, dense_left = dense_right[:tok_count], dense_left[:tok_count]
        dense_right, dense_left = to_right(dense_right), to_left(dense_left)
    dense_rows = put(dense_rows, dense_right, half, 0)
    dense_rows = put(dense_rows, dense_left, half, tok_count)

    far = lax.ppermute(near, "outer", [(i, i ^ 1) for i in range(n_outer)])
    dense = dense_up(near)
    rows, dense = lax.optimization_barrier((rows, dense))
    w_in, w_out = expert_in[0], expert_out[0]
    pre = dot(rows[:slots], w_in)
    grad = contract_last(rows[slots:], w_out)
    back = contract_last((grad * gelu_prime(pre)).astype(bf16), w_in).astype(bf16)
    hidden = gelu_value(pre).astype(bf16)

    def part_out(offset):
        weights = lax.dynamic_slice(w_out, (zero, start_of(offset)), (w_out.shape[0], feat))
        return dot(hidden, weights)

    mid = slots // 2
    first = part_out(half).astype(bf16)
    back, first, far, dense_rows = lax.optimization_barrier((back, first, far, dense_rows))
    sum_back = lax.psum_scatter(back, "node", scatter_dimension=1, tiled=True)
    right, left = to_right(first[:mid]), to_left(first[mid:])
    for step in range(half - 1, 0, -1):
        ro, lo = part_out(step), part_out(-step)
        if step == half - 1:
            ro = jnp.concatenate([ro[:mid] + right.astype(f32), ro[mid:]], axis=0)
            lo = jnp.concatenate([lo[:mid], lo[mid:] + left.astype(f32)], axis=0)
        else:
            ro, lo = ro + right.astype(f32), lo + left.astype(f32)
        right, left = ro.astype(bf16), lo.astype(bf16)
        if step == half - 1:
            wi_n, wo_n, hid_n, dpre_n = dense
            wi_f, wo_f, hid_f, dpre_f = dense_up(far)
            right, left, hid_f, dpre_f = lax.optimization_barrier((right, left, hid_f, dpre_f))
        elif step == half - 2:
            dense = jnp.concatenate(
                [
                    contract_last(hid_n, wo_n) + contract_last(hid_f, wo_f),
                    contract_last(dpre_n, wi_n) + contract_last(dpre_f, wi_f),
                ],
                axis=0,
            ).astype(bf16)
            right, left, dense = lax.optimization_barrier((right, left, dense))
        right, left = to_right(right), to_left(left)
    sum_out = (part_out(0) + right.astype(f32) + left.astype(f32)).astype(bf16)
    dense_sum = lax.psum_scatter(dense, "node", scatter_dimension=1, tiled=True)

    reply = jnp.concatenate(
        [
            sum_out.reshape(n_outer, capacity, feat),
            sum_back.reshape(n_outer, capacity, feat),
        ],
        axis=1,
    )
    reply = lax.all_to_all(reply, "outer", split_axis=0, concat_axis=0, tiled=True)

    picked_out = lax.dot_general(
        place,
        reply[:, :capacity].reshape(slots, feat),
        (((0,), (0,)), ((), ())),
        preferred_element_type=f32,
    )
    picked_back = lax.dot_general(
        place,
        reply[:, capacity:].reshape(slots, feat),
        (((0,), (0,)), ((), ())),
        preferred_element_type=f32,
    )
    scale = gate[:, None]
    mixed = tokens.astype(f32) + scale * picked_out
    input_grad = cotangent.astype(f32) + scale * picked_back
    mixed, input_grad = lax.optimization_barrier((mixed, input_grad))
    mixed = mixed + dense_sum[:tok_count].astype(f32)
    input_grad = input_grad + dense_sum[tok_count:].astype(f32)
    return mixed.astype(bf16), input_grad.astype(bf16)


def solution(mesh):
    placed = (
        P("outer", "node"),
        P("outer", "node"),
        P("outer"),
        P("outer", None),
        P("outer", "node"),
        P("node", "outer"),
        P("outer", None, "node"),
        P("outer", "node", None),
    )
    return jax.shard_map(
        body,
        mesh=mesh,
        in_specs=placed,
        out_specs=(P("outer", "node"), P("outer", "node")),
        check_vma=False,
    )
```
